32 devices in a mesh: row: 8 (over y, x, core), col: 4 (over z).
Axes of the slice: x: 2, y: 2, z: 4, core: 2. Of those that a mesh axis runs over, the one named last changes fastest.
Arguments:
- panel: float32 [32768, 256], P(('row', 'col')), may hold values from -8 to 8
- diag_inverse: float32 [256, 256], replicated
- tiles: bfloat16 [8704, 256, 256], P(('row', 'col')), may hold values from -6 to 6
- tile_map: int32 [8704, 2], P(('row', 'col')), may hold values from -1 to 31, as said below
- send_list: int32 [256], P(('row', 'col')), may hold values from -1 to 271, as said below
- place_list: int32 [8448], P(('row', 'col')), may hold values from -1 to 279, as said below
Outputs:
- factor_panel: float32 [32768, 256], P(('row', 'col'))
- balanced: bfloat16 [8448, 256, 256], P(('row', 'col'))
The draws below stay inside these ranges and needn't reach their ends.
Inputs may be any that keep to these rules, and one draw needn't show every extreme that they name: `tile_map`: each lower tile (I >= J) owned block-cyclically by a device appears in exactly one of its slots, in a drawn order; its other slots hold -1 in both entries. `send_list`: entries of a device name distinct live slots of that device, those it hands to its partner; unused entries are -1 and stand after the used ones. `place_list`: over a device's 264 entries, every live slot it does not hand over and every used send entry of its partner appear exactly once, in a drawn order; the rest are -1.
All inputs are finite; a program needn't handle non-finite values.
Results may differ from the reference program's by a relative error of at most 0.0051.
Values may be sent and summed in bfloat16 or wider, within the bound.
No kernel may reach another device: no remote copies, remote signals or barrier semaphores. Data moves between devices by JAX's collectives and lax.ppermute only.
A program may use at most 256 MiB of HBM per device.

```python
import math
import jax
import jax.numpy as jnp
from jax import lax

TILE = 256
TILES = 128
ORDER = 32768
ROW_TILES = 16
COL_TILES = 32
SLOTS = 272
HELD = 264
MOVED = 8
N_ROW = 8
N_COL = 4
DEVICES = 32


def device_layout(key):
    base_key = jax.random.fold_in(key, 1009)
    cell_total = ROW_TILES * COL_TILES
    row_ids = jnp.arange(ROW_TILES, dtype=jnp.int32)[:, None]
    col_ids = jnp.arange(COL_TILES, dtype=jnp.int32)[None, :]
    slot_ids = jnp.arange(SLOTS, dtype=jnp.int32)

    def one_device(dev_key, rank_row, rank_col):
        key_cells, key_slots, key_live = jax.random.split(dev_key, 3)
        is_alive = (row_ids * N_ROW + rank_row >= col_ids * N_COL + rank_col).reshape(-1).astype(jnp.int32)
        scores = (1 - is_alive) * cell_total + jax.random.permutation(key_cells, cell_total).astype(jnp.int32)
        cell_ids = jnp.argsort(scores, stable=True)[:SLOTS].astype(jnp.int32)
        live_count = jnp.sum(is_alive)
        cell_ids = jnp.where(slot_ids < live_count, cell_ids, -1)
        cell_ids = jax.random.permutation(key_slots, cell_ids)
        tile_rows = jnp.where(cell_ids >= 0, cell_ids // COL_TILES, -1)
        tile_cols = jnp.where(cell_ids >= 0, cell_ids % COL_TILES, -1)
        slot_scores = jnp.where(cell_ids >= 0, jax.random.permutation(key_live, SLOTS).astype(jnp.int32), SLOTS + slot_ids)
        live_slots = jnp.argsort(slot_scores, stable=True).astype(jnp.int32)
        return (jnp.stack([tile_rows, tile_cols], 1), live_count, live_slots)
    dev_ids = jnp.arange(DEVICES, dtype=jnp.int32)
    rank_rows = dev_ids // N_COL
    rank_cols = dev_ids % N_COL
    dev_keys = jax.random.split(base_key, DEVICES)
    tile_maps, live_counts, live_slots = jax.vmap(one_device)(dev_keys, rank_rows, rank_cols)
    excess = jnp.maximum(live_counts - HELD, 0)
    partner = (N_ROW - 1 - rank_rows) * N_COL + rank_cols
    incoming = excess[partner]
    kept_count = live_counts - excess
    move_ids = jnp.arange(MOVED, dtype=jnp.int32)[None, :]
    picks = jnp.clip(kept_count[:, None] + move_ids, 0, SLOTS - 1)
    send_rows = jnp.where(move_ids < excess[:, None], jnp.take_along_axis(live_slots, picks, 1), -1)
    held_ids = jnp.arange(HELD, dtype=jnp.int32)[None, :]
    first_part = jnp.take_along_axis(live_slots, jnp.clip(held_ids, 0, SLOTS - 1), 1)
    later_part = jnp.where(held_ids < (kept_count + incoming)[:, None], SLOTS + held_ids - kept_count[:, None], -1)
    place_rows = jnp.where(held_ids < kept_count[:, None], first_part, later_part)
    place_keys = jax.random.split(jax.random.fold_in(base_key, 2), DEVICES)

    def mix_row(row_key, row_values):
        return jax.random.permutation(row_key, row_values)
    place_rows = jax.vmap(mix_row)(place_keys, place_rows)
    return (tile_maps.reshape(DEVICES * SLOTS, 2).astype(jnp.int32), send_rows.reshape(-1).astype(jnp.int32), place_rows.reshape(-1).astype(jnp.int32))


def draw_tile_map(key, part):
    return device_layout(key)[0]


def draw_send_list(key, part):
    return device_layout(key)[1]


def draw_place_list(key, part):
    return device_layout(key)[2]


def draw_diag_inverse(key, part):
    key_diag, key_off = jax.random.split(jax.random.fold_in(key, 3))
    row_ids = jnp.arange(TILE)[:, None]
    col_ids = jnp.arange(TILE)[None, :]
    diagonal = jax.random.uniform(key_diag, (TILE,), jnp.float32, 0.12, 0.25)
    lower_part = jax.random.normal(key_off, (TILE, TILE), jnp.float32) * (0.12 / math.sqrt(TILE))
    lower_part = jnp.where(row_ids > col_ids, lower_part, 0.0)
    return (lower_part + jnp.diag(diagonal)).astype(jnp.float32)


def block_scale(own_key, extent, cuts, least, high):
    loudness, own = 1.0, jax.random.fold_in(own_key, 6)
    for axis_at, parts in cuts:
        steps = jnp.exp(jax.random.uniform(jax.random.fold_in(own, axis_at), (parts,), jnp.float32, least / len(cuts), high / len(cuts)))
        loudness = loudness * jnp.repeat(steps, extent[axis_at] // parts).reshape([-1 if axis == axis_at else 1 for axis in range(len(extent))])
    return loudness


def normal_values(own_key, extent, spread, most, shards=(), kind=jnp.bfloat16):
    loudness = block_scale(own_key, extent, shards, -0.22, 0.18) if shards else 1.0
    values = jax.random.normal(own_key, extent, jnp.float32) * spread * loudness
    return jnp.minimum(jnp.maximum(values, -most), most).astype(kind)


def setup_inputs(seed: int = 0) -> dict:
    keys = jax.random.split(jax.random.key(seed), 7)
    panel = normal_values(keys[0], (ORDER, TILE), 1.5, 8.0, ((0, 32),), jnp.float32)
    diag_inverse = draw_diag_inverse(jax.random.fold_in(keys[6], 71), 0)
    tiles = normal_values(keys[2], (DEVICES * SLOTS, TILE, TILE), 1.0, 6.0, ((0, 32),))
    tile_map = draw_tile_map(jax.random.fold_in(keys[6], 71), 0)
    send_list = draw_send_list(jax.random.fold_in(keys[6], 71), 0)
    place_list = draw_place_list(jax.random.fold_in(keys[6], 71), 0)
    return {"panel": panel, "diag_inverse": diag_inverse, "tiles": tiles, "tile_map": tile_map, "send_list": send_list, "place_list": place_list}


def reference(panel, diag_inverse, tiles, tile_map, send_list, place_list):
    factor = jnp.dot(panel, diag_inverse.T, precision=lax.Precision.HIGHEST, preferred_element_type=jnp.float32)
    factor_tiles = factor.astype(jnp.bfloat16).reshape(TILES, TILE, TILE)
    send_rows = send_list.reshape(DEVICES, MOVED)
    place_rows = place_list.reshape(DEVICES, HELD)

    def one_device(device):
        rank_row = device // N_COL
        rank_col = device % N_COL
        partner = (N_ROW - 1 - rank_row) * N_COL + rank_col
        source = place_rows[device]
        remote = source >= SLOTS
        far_index = jnp.clip(source - SLOTS, 0, MOVED - 1)
        far_slot = send_rows[partner][far_index]
        owner = jnp.where(remote, partner, device)
        slot_index = jnp.clip(jnp.where(remote, far_slot, source), 0, SLOTS - 1)
        flat_index = (owner * SLOTS + slot_index).astype(jnp.int32)
        raw_tiles = tiles[flat_index]
        cell_rows = tile_map[flat_index]
        owner_row = owner // N_COL
        row_local = jnp.clip(cell_rows[:, 0], 0, ROW_TILES - 1)
        col_local = jnp.clip(cell_rows[:, 1], 0, COL_TILES - 1)
        left_tiles = factor_tiles[(owner_row * ROW_TILES + row_local).astype(jnp.int32)]
        col_global = col_local * N_COL + rank_col
        right_tiles = factor_tiles[((col_global % N_ROW) * ROW_TILES + col_global // N_ROW).astype(jnp.int32)]
        product = jnp.einsum("kil,kjl->kij", left_tiles.astype(jnp.float32), right_tiles.astype(jnp.float32))
        result = (raw_tiles.astype(jnp.float32) - product).astype(jnp.bfloat16)
        return jnp.where((source >= 0)[:, None, None], result, jnp.zeros((), jnp.bfloat16))

    balanced = lax.map(one_device, jnp.arange(DEVICES, dtype=jnp.int32))
    return factor, balanced.reshape(DEVICES * HELD, TILE, TILE)
```

```python
import functools
import jax
import jax.numpy as jnp
from jax import lax
from jax.experimental import pallas as pl
from jax.experimental.pallas import tpu as pltpu
from jax.sharding import PartitionSpec as P

AXES = ("row", "col")
RING = 6
VMEM_LIMIT = 24 * 1024 * 1024


def tied(value, *others):
    return lax.optimization_barrier((value,) + others)[0]


def across(value, row, column, row_count, col_count):
    known = col_count - 1
    for bit in range(col_count.bit_length() - 2, 0, -1):
        received = lax.ppermute(value, AXES, spread_pairs(bit, known, row_count, col_count))
        known &= ~(1 << bit)
        value = jnp.where(((row ^ column) >> bit) & 1 == 0, value, received)
    return value


def exchanged(value, known, row_count, col_count):
    pieces = [value]
    for bit in range(col_count.bit_length() - 1, row_count.bit_length() - 1):
        pieces = pieces + [
            lax.ppermute(piece, AXES, spread_pairs(bit, known, row_count, col_count)) for piece in pieces
        ]
    return pieces


def spread_pairs(bit, known, row_count, col_count):
    chosen = []
    for source in range(row_count):
        for place in range(col_count):
            if (source ^ place) & known == 0:
                chosen.append((source * col_count + place, (source ^ (1 << bit)) * col_count + place))
    return chosen


def gather_and_spread(half, early, row, column, row_count, col_count):
    sizes = (row_count, col_count)

    def forward(part):
        value = across(part, row, column, *sizes)
        return exchanged(value, 1, *sizes)

    def to_other_core(near):
        return lax.ppermute(near, AXES, spread_pairs(0, 1, *sizes))

    def z_pairs(hops, wanted):
        return [
            (place * col_count + source, place * col_count + target)
            for place in range(row_count)
            for source, target in hops
            if (place % col_count == target) == wanted
        ]

    parts = [half]
    for mask in range(1, min(col_count, 3)):
        parts.append(lax.ppermute(half, "col", [(place, place ^ mask) for place in range(col_count)]))
    pieces = [forward(tied(half, early))]
    if col_count == 4:
        outer, inner = [(1, 0), (2, 3)], [(1, 2), (2, 1)]
        at_end = (column == 0) | (column == 3)
        near = [jnp.concatenate(pieces[0], 0)]
        middle = lax.ppermute(tied(half, parts[2]), AXES, z_pairs(inner, True))
        onward = lax.ppermute(tied(parts[2], pieces[0][-1], parts[1]), AXES, z_pairs(outer, True))
        first = jnp.where(at_end, onward, middle)
        turned = jnp.concatenate(exchanged(parts[2], col_count - 1, *sizes), 0)
        pieces.append(forward(parts[1]))
        middle = lax.ppermute(tied(half, parts[1], parts[2]), AXES, z_pairs(inner, False))
        onward = lax.ppermute(tied(parts[2], parts[1]), AXES, z_pairs(outer, False))
        near.append(jnp.concatenate(pieces[1], 0))
        near.append(across(tied(turned, first), row, column, *sizes))
        near.append(jnp.concatenate(forward(first), 0))
        parts += [first, onward, middle]
        near[1] = tied(near[1], onward, middle)
        near[3] = tied(near[3], near[2])
        far = [to_other_core(held) for held in near]
    else:
        for mask in range(len(parts), col_count):
            parts.append(lax.ppermute(half, "col", [(place, place ^ mask) for place in range(col_count)]))
        pieces += [forward(part) for part in parts[1:]]
        near = [jnp.concatenate(held, 0) for held in pieces]
        far = [to_other_core(held) for held in near]
    return parts, near, far


def renew_kernel(sizes, source_list, cell_list, *refs):
    col_count, groups, row_local, part_rows, slot_count, count, batch, ring = sizes
    part_count = len(refs) - 2 * col_count - 10
    row_parts, refs = refs[:part_count], refs[part_count:]
    col_near, refs = refs[:col_count], refs[col_count:]
    col_far, refs = refs[:col_count], refs[col_count:]
    tiles, out, row_buf, col_buf, in_buf, out_buf, row_sem, col_sem, in_sem, out_sem = refs
    tile_size = tiles.shape[1]
    steps = count // batch
    row = lax.axis_index("row")
    column = lax.axis_index("col")

    def fetch(step, slot):
        for t in range(batch):
            chosen = jnp.clip(source_list[step * batch + t], 0, slot_count - 1)
            pltpu.make_async_copy(tiles.at[chosen], in_buf.at[slot, t], in_sem.at[slot]).start()

    def cell(index):
        chosen = jnp.clip(source_list[index], 0, slot_count - 1)
        at_col = jnp.maximum(cell_list[1, chosen], 0)
        return jnp.maximum(cell_list[0, chosen], 0), lax.rem(at_col, groups), at_col // groups

    def stage(source, target, at, sem):
        pltpu.make_async_copy(source, target.at[pl.ds(pl.multiple_of(at, part_rows), part_rows)], sem).start()

    leads = lax.rem(row, col_count) == column
    at_end = (column == 0) | (column == col_count - 1)
    cases = (leads, jnp.logical_not(leads) & at_end, jnp.logical_not(leads | at_end))
    row_entries = [(entry, mask, None) for mask, entry in enumerate(row_parts[:col_count])]
    if part_count > col_count:
        last = col_count - 1
        row_entries = row_entries[:last] + [(entry, last, case) for entry, case in zip(row_parts[last:], cases)]
    is_near = (row ^ column) & 1 == 0

    def stage_all():
        for entry, mask, case in row_entries:
            @pl.when(True if case is None else case)
            def _(entry=entry, mask=mask):
                stage(entry, row_buf, (column ^ mask) * part_rows, row_sem)

        for held, wanted in ((col_near, is_near), (col_far, jnp.logical_not(is_near))):
            @pl.when(wanted)
            def _(held=held):
                for mask in range(col_count):
                    for piece in range(groups):
                        group = (row // col_count) ^ piece
                        at = (group * col_count + (column ^ mask)) * part_rows
                        stage(held[mask].at[pl.ds(piece * part_rows, part_rows)], col_buf, at, col_sem)

    early = min(2, ring, steps)
    for step in range(early):
        fetch(step, step)
    stage_all()
    for step in range(early, min(ring, steps)):
        fetch(step, step)
    pltpu.make_async_copy(row_buf, row_buf, row_sem).wait()
    pltpu.make_async_copy(col_buf, col_buf, col_sem).wait()

    def body(step, carry):
        slot = lax.rem(step, ring)
        pltpu.make_async_copy(in_buf.at[slot], in_buf.at[slot], in_sem.at[slot]).wait()

        @pl.when(step >= ring)
        def _():
            pltpu.make_async_copy(out_buf.at[slot], out_buf.at[slot], out_sem.at[slot]).wait()

        for t in range(batch):
            source = source_list[step * batch + t]
            at_row, group, at_col = cell(step * batch + t)
            at_flat = group * row_local + at_col
            left = row_buf[pl.ds(pl.multiple_of(at_row * tile_size, tile_size), tile_size), :]
            right = col_buf[pl.ds(pl.multiple_of(at_flat * tile_size, tile_size), tile_size), :]
            product = lax.dot_general(left, right, (((1,), (1,)), ((), ())), preferred_element_type=jnp.float32)
            fresh = in_buf[slot, t].astype(jnp.float32) - product
            out_buf[slot, t] = jnp.where(source >= 0, fresh, 0.0).astype(jnp.bfloat16)
        pltpu.make_async_copy(out_buf.at[slot], out.at[pl.ds(step * batch, batch)], out_sem.at[slot]).start()

        @pl.when(step + ring < steps)
        def _():
            fetch(step + ring, slot)

        return carry

    lax.fori_loop(0, steps, body, 0)
    for step in range(max(0, steps - ring), steps):
        slot = step % ring
        pltpu.make_async_copy(out_buf.at[slot], out_buf.at[slot], out_sem.at[slot]).wait()


def renew(source_list, cell_list, row_parts, col_near, col_far, tiles, groups, batch_most):
    slot_count, tile_size, _ = tiles.shape
    count = source_list.shape[0]
    part_rows = row_parts[0].shape[0]
    col_count = len(col_near)
    row_local = col_count * part_rows // tile_size
    batch = max(size for size in range(1, batch_most + 1) if count % size == 0)
    ring = min(RING, count // batch)
    sizes = (col_count, groups, row_local, part_rows, slot_count, count, batch, ring)
    operands = list(row_parts) + list(col_near) + list(col_far) + [tiles]
    tile_bytes = tile_size * tile_size * 2
    return pl.pallas_call(
        functools.partial(renew_kernel, sizes),
        out_shape=jax.ShapeDtypeStruct((count, tile_size, tile_size), jnp.bfloat16),
        grid_spec=pltpu.PrefetchScalarGridSpec(
            num_scalar_prefetch=2,
            grid=(),
            in_specs=[pl.BlockSpec(memory_space=pl.ANY)] * len(operands),
            out_specs=pl.BlockSpec(memory_space=pl.ANY),
            scratch_shapes=[
                pltpu.VMEM((row_local * tile_size, tile_size), jnp.bfloat16),
                pltpu.VMEM((groups * row_local * tile_size, tile_size), jnp.bfloat16),
                pltpu.VMEM((ring, batch, tile_size, tile_size), jnp.bfloat16),
                pltpu.VMEM((ring, batch, tile_size, tile_size), jnp.bfloat16),
                pltpu.SemaphoreType.DMA,
                pltpu.SemaphoreType.DMA,
                pltpu.SemaphoreType.DMA((ring,)),
                pltpu.SemaphoreType.DMA((ring,)),
            ],
        ),
        compiler_params=pltpu.CompilerParams(vmem_limit_bytes=VMEM_LIMIT),
        cost_estimate=pl.CostEstimate(
            flops=2 * count * tile_size**3,
            bytes_accessed=2 * count * tile_bytes + (1 + groups) * row_local * tile_bytes,
            transcendentals=0,
        ),
    )(source_list, cell_list, *operands)


def place_kernel(places, incoming, held, out, sem):
    del held
    count = incoming.shape[0]
    for index in range(count):
        @pl.when(places[index] >= 0)
        def _():
            pltpu.make_async_copy(incoming.at[index], out.at[places[index]], sem.at[index]).start()
    for index in range(count):
        @pl.when(places[index] >= 0)
        def _():
            pltpu.make_async_copy(incoming.at[index], out.at[places[index]], sem.at[index]).wait()


def place(places, incoming, held):
    return pl.pallas_call(
        place_kernel,
        out_shape=jax.ShapeDtypeStruct(held.shape, held.dtype),
        grid_spec=pltpu.PrefetchScalarGridSpec(
            num_scalar_prefetch=1,
            grid=(),
            in_specs=[pl.BlockSpec(memory_space=pltpu.VMEM), pl.BlockSpec(memory_space=pl.ANY)],
            out_specs=pl.BlockSpec(memory_space=pl.ANY),
            scratch_shapes=[pltpu.SemaphoreType.DMA((incoming.shape[0],))],
        ),
        input_output_aliases={2: 0},
        compiler_params=pltpu.CompilerParams(vmem_limit_bytes=4 * 1024 * 1024),
    )(places, incoming, held)


def shards(panel, diag_inverse, tiles, tile_map, send_list, place_list):
    slot_count = tiles.shape[0]
    move_count = send_list.shape[0]
    row_count = lax.axis_size("row")
    col_count = lax.axis_size("col")
    row = lax.axis_index("row")
    column = lax.axis_index("col")
    groups = row_count // col_count
    factor = jnp.dot(
        panel, diag_inverse.T, precision=lax.Precision.HIGH, preferred_element_type=jnp.float32
    )
    half = factor.astype(jnp.bfloat16)

    wanted = slot_count + jnp.arange(move_count, dtype=jnp.int32)
    spots = jnp.arange(place_list.shape[0], dtype=jnp.int32)
    places = jnp.max(jnp.where(place_list[None, :] == wanted[:, None], spots[None, :], -1), axis=1)

    row_parts, near, far = gather_and_spread(half, places, row, column, row_count, col_count)

    renewing = functools.partial(
        renew, cell_list=tile_map.T, row_parts=row_parts, col_near=near, col_far=far,
        tiles=tiles, groups=groups,
    )
    outgoing = renewing(send_list, batch_most=2)
    incoming = lax.ppermute(outgoing, "row", [(source, row_count - 1 - source) for source in range(row_count)])
    held = renewing(place_list, batch_most=8)
    balanced = place(places, incoming, held)
    return (factor, balanced)


def solution(mesh):
    in_specs = (
        P(("row", "col"), None),
        P(),
        P(("row", "col"), None, None),
        P(("row", "col"), None),
        P(("row", "col")),
        P(("row", "col")),
    )
    out_specs = (P(("row", "col"), None), P(("row", "col"), None, None))
    return jax.shard_map(shards, mesh=mesh, in_specs=in_specs, out_specs=out_specs, check_vma=False)
```

```python
import functools
import jax
import jax.numpy as jnp
from jax import lax
from jax.experimental import pallas as pl
from jax.experimental.pallas import tpu as pltpu
from jax.sharding import PartitionSpec as P

AXES = ("row", "col")
RING = 6
VMEM_LIMIT = 24 * 1024 * 1024


def tied(value, *others):
    return lax.optimization_barrier((value,) + others)[0]


def across(value, row, column, row_count, col_count):
    known = col_count - 1
    for bit in range(col_count.bit_length() - 2, 0, -1):
        received = lax.ppermute(value, AXES, spread_pairs(bit, known, row_count, col_count))
        known &= ~(1 << bit)
        value = jnp.where(((row ^ column) >> bit) & 1 == 0, value, received)
    return value


def exchanged(value, known, row_count, col_count):
    pieces = [value]
    for bit in range(col_count.bit_length() - 1, row_count.bit_length() - 1):
        pieces = pieces + [
            lax.ppermute(piece, AXES, spread_pairs(bit, known, row_count, col_count)) for piece in pieces
        ]
    return pieces


def spread_pairs(bit, known, row_count, col_count):
    chosen = []
    for source in range(row_count):
        for place in range(col_count):
            if (source ^ place) & known == 0:
                chosen.append((source * col_count + place, (source ^ (1 << bit)) * col_count + place))
    return chosen


def gather_and_spread(half, early, row, column, row_count, col_count):
    sizes = (row_count, col_count)

    def forward(part):
        value = across(part, row, column, *sizes)
        return exchanged(value, 1, *sizes)

    def to_other_core(near):
        return lax.ppermute(near, AXES, spread_pairs(0, 1, *sizes))

    def z_pairs(hops, wanted):
        return [
            (place * col_count + source, place * col_count + target)
            for place in range(row_count)
            for source, target in hops
            if (place % col_count == target) == wanted
        ]

    parts = [half]
    for mask in range(1, min(col_count, 3)):
        parts.append(lax.ppermute(half, "col", [(place, place ^ mask) for place in range(col_count)]))
    pieces = [forward(tied(half, early))]
    if col_count == 4:
        outer, inner = [(1, 0), (2, 3)], [(1, 2), (2, 1)]
        at_end = (column == 0) | (column == 3)
        near = [jnp.concatenate(pieces[0], 0)]
        middle = lax.ppermute(tied(half, parts[2]), AXES, z_pairs(inner, True))
        onward = lax.ppermute(parts[2], AXES, z_pairs(outer, True))
        first = jnp.where(at_end, onward, middle)
        turned = jnp.concatenate(exchanged(tied(parts[2], parts[1], pieces[0][-1]), col_count - 1, *sizes), 0)
        pieces.append(forward(parts[1]))
        middle = lax.ppermute(tied(half, parts[1], parts[2]), AXES, z_pairs(inner, False))
        onward = lax.ppermute(tied(parts[2], parts[1]), AXES, z_pairs(outer, False))
        near.append(jnp.concatenate(pieces[1], 0))
        near.append(across(tied(turned, first), row, column, *sizes))
        near.append(jnp.concatenate(forward(first), 0))
        parts += [first, onward, middle]
        near[1] = tied(near[1], onward, middle)
        near[3] = tied(near[3], near[2])
        far = [to_other_core(held) for held in near]
    else:
        for mask in range(len(parts), col_count):
            parts.append(lax.ppermute(half, "col", [(place, place ^ mask) for place in range(col_count)]))
        pieces += [forward(part) for part in parts[1:]]
        near = [jnp.concatenate(held, 0) for held in pieces]
        far = [to_other_core(held) for held in near]
    return parts, near, far


def renew_kernel(sizes, source_list, cell_list, *refs):
    col_count, groups, row_local, part_rows, slot_count, count, batch, ring = sizes
    part_count = len(refs) - 2 * col_count - 10
    row_parts, refs = refs[:part_count], refs[part_count:]
    col_near, refs = refs[:col_count], refs[col_count:]
    col_far, refs = refs[:col_count], refs[col_count:]
    tiles, out, row_buf, col_buf, in_buf, out_buf, row_sem, col_sem, in_sem, out_sem = refs
    tile_size = tiles.shape[1]
    steps = count // batch
    row = lax.axis_index("row")
    column = lax.axis_index("col")

    def fetch(step, slot):
        for t in range(batch):
            chosen = jnp.clip(source_list[step * batch + t], 0, slot_count - 1)
            pltpu.make_async_copy(tiles.at[chosen], in_buf.at[slot, t], in_sem.at[slot]).start()

    def cell(index):
        chosen = jnp.clip(source_list[index], 0, slot_count - 1)
        at_col = jnp.maximum(cell_list[1, chosen], 0)
        return jnp.maximum(cell_list[0, chosen], 0), lax.rem(at_col, groups), at_col // groups

    def stage(source, target, at, sem):
        pltpu.make_async_copy(source, target.at[pl.ds(pl.multiple_of(at, part_rows), part_rows)], sem).start()

    leads = lax.rem(row, col_count) == column
    at_end = (column == 0) | (column == col_count - 1)
    cases = (leads, jnp.logical_not(leads) & at_end, jnp.logical_not(leads | at_end))
    row_entries = [(entry, mask, None) for mask, entry in enumerate(row_parts[:col_count])]
    if part_count > col_count:
        last = col_count - 1
        row_entries = row_entries[:last] + [(entry, last, case) for entry, case in zip(row_parts[last:], cases)]
    is_near = (row ^ column) & 1 == 0

    def stage_all():
        for entry, mask, case in row_entries:
            @pl.when(True if case is None else case)
            def _(entry=entry, mask=mask):
                stage(entry, row_buf, (column ^ mask) * part_rows, row_sem)

        for held, wanted in ((col_near, is_near), (col_far, jnp.logical_not(is_near))):
            @pl.when(wanted)
            def _(held=held):
                for mask in range(col_count):
                    for piece in range(groups):
                        group = (row // col_count) ^ piece
                        at = (group * col_count + (column ^ mask)) * part_rows
                        stage(held[mask].at[pl.ds(piece * part_rows, part_rows)], col_buf, at, col_sem)

    early = min(2, ring, steps)
    for step in range(early):
        fetch(step, step)
    stage_all()
    for step in range(early, min(ring, steps)):
        fetch(step, step)
    pltpu.make_async_copy(row_buf, row_buf, row_sem).wait()
    pltpu.make_async_copy(col_buf, col_buf, col_sem).wait()

    def body(step, carry):
        slot = lax.rem(step, ring)
        pltpu.make_async_copy(in_buf.at[slot], in_buf.at[slot], in_sem.at[slot]).wait()

        @pl.when(step >= ring)
        def _():
            pltpu.make_async_copy(out_buf.at[slot], out_buf.at[slot], out_sem.at[slot]).wait()

        for t in range(batch):
            source = source_list[step * batch + t]
            at_row, group, at_col = cell(step * batch + t)
            at_flat = group * row_local + at_col
            left = row_buf[pl.ds(pl.multiple_of(at_row * tile_size, tile_size), tile_size), :]
            right = col_buf[pl.ds(pl.multiple_of(at_flat * tile_size, tile_size), tile_size), :]
            product = lax.dot_general(left, right, (((1,), (1,)), ((), ())), preferred_element_type=jnp.float32)
            fresh = in_buf[slot, t].astype(jnp.float32) - product
            out_buf[slot, t] = jnp.where(source >= 0, fresh, 0.0).astype(jnp.bfloat16)
        pltpu.make_async_copy(out_buf.at[slot], out.at[pl.ds(step * batch, batch)], out_sem.at[slot]).start()

        @pl.when(step + ring < steps)
        def _():
            fetch(step + ring, slot)

        return carry

    lax.fori_loop(0, steps, body, 0)
    for step in range(max(0, steps - ring), steps):
        slot = step % ring
        pltpu.make_async_copy(out_buf.at[slot], out_buf.at[slot], out_sem.at[slot]).wait()


def renew(source_list, cell_list, row_parts, col_near, col_far, tiles, groups, batch_most):
    slot_count, tile_size, _ = tiles.shape
    count = source_list.shape[0]
    part_rows = row_parts[0].shape[0]
    col_count = len(col_near)
    row_local = col_count * part_rows // tile_size
    batch = max(size for size in range(1, batch_most + 1) if count % size == 0)
    ring = min(RING, count // batch)
    sizes = (col_count, groups, row_local, part_rows, slot_count, count, batch, ring)
    operands = list(row_parts) + list(col_near) + list(col_far) + [tiles]
    tile_bytes = tile_size * tile_size * 2
    return pl.pallas_call(
        functools.partial(renew_kernel, sizes),
        out_shape=jax.ShapeDtypeStruct((count, tile_size, tile_size), jnp.bfloat16),
        grid_spec=pltpu.PrefetchScalarGridSpec(
            num_scalar_prefetch=2,
            grid=(),
            in_specs=[pl.BlockSpec(memory_space=pl.ANY)] * len(operands),
            out_specs=pl.BlockSpec(memory_space=pl.ANY),
            scratch_shapes=[
                pltpu.VMEM((row_local * tile_size, tile_size), jnp.bfloat16),
                pltpu.VMEM((groups * row_local * tile_size, tile_size), jnp.bfloat16),
                pltpu.VMEM((ring, batch, tile_size, tile_size), jnp.bfloat16),
                pltpu.VMEM((ring, batch, tile_size, tile_size), jnp.bfloat16),
                pltpu.SemaphoreType.DMA,
                pltpu.SemaphoreType.DMA,
                pltpu.SemaphoreType.DMA((ring,)),
                pltpu.SemaphoreType.DMA((ring,)),
            ],
        ),
        compiler_params=pltpu.CompilerParams(vmem_limit_bytes=VMEM_LIMIT),
        cost_estimate=pl.CostEstimate(
            flops=2 * count * tile_size**3,
            bytes_accessed=2 * count * tile_bytes + (1 + groups) * row_local * tile_bytes,
            transcendentals=0,
        ),
    )(source_list, cell_list, *operands)


def place_kernel(places, incoming, held, out, sem):
    del held
    count = incoming.shape[0]
    for index in range(count):
        @pl.when(places[index] >= 0)
        def _():
            pltpu.make_async_copy(incoming.at[index], out.at[places[index]], sem.at[index]).start()
    for index in range(count):
        @pl.when(places[index] >= 0)
        def _():
            pltpu.make_async_copy(incoming.at[index], out.at[places[index]], sem.at[index]).wait()


def place(places, incoming, held):
    return pl.pallas_call(
        place_kernel,
        out_shape=jax.ShapeDtypeStruct(held.shape, held.dtype),
        grid_spec=pltpu.PrefetchScalarGridSpec(
            num_scalar_prefetch=1,
            grid=(),
            in_specs=[pl.BlockSpec(memory_space=pltpu.VMEM), pl.BlockSpec(memory_space=pl.ANY)],
            out_specs=pl.BlockSpec(memory_space=pl.ANY),
            scratch_shapes=[pltpu.SemaphoreType.DMA((incoming.shape[0],))],
        ),
        input_output_aliases={2: 0},
        compiler_params=pltpu.CompilerParams(vmem_limit_bytes=4 * 1024 * 1024),
    )(places, incoming, held)


def shards(panel, diag_inverse, tiles, tile_map, send_list, place_list):
    slot_count = tiles.shape[0]
    move_count = send_list.shape[0]
    row_count = lax.axis_size("row")
    col_count = lax.axis_size("col")
    row = lax.axis_index("row")
    column = lax.axis_index("col")
    groups = row_count // col_count
    factor = jnp.dot(
        panel, diag_inverse.T, precision=lax.Precision.HIGH, preferred_element_type=jnp.float32
    )
    half = factor.astype(jnp.bfloat16)

    wanted = slot_count + jnp.arange(move_count, dtype=jnp.int32)
    spots = jnp.arange(place_list.shape[0], dtype=jnp.int32)
    places = jnp.max(jnp.where(place_list[None, :] == wanted[:, None], spots[None, :], -1), axis=1)

    row_parts, near, far = gather_and_spread(half, places, row, column, row_count, col_count)

    renewing = functools.partial(
        renew, cell_list=tile_map.T, row_parts=row_parts, col_near=near, col_far=far,
        tiles=tiles, groups=groups,
    )
    outgoing = renewing(send_list, batch_most=2)
    incoming = lax.ppermute(outgoing, "row", [(source, row_count - 1 - source) for source in range(row_count)])
    held = renewing(place_list, batch_most=8)
    balanced = place(places, incoming, held)
    return (factor, balanced)


def solution(mesh):
    in_specs = (
        P(("row", "col"), None),
        P(),
        P(("row", "col"), None, None),
        P(("row", "col"), None),
        P(("row", "col")),
        P(("row", "col")),
    )
    out_specs = (P(("row", "col"), None), P(("row", "col"), None, None))
    return jax.shard_map(shards, mesh=mesh, in_specs=in_specs, out_specs=out_specs, check_vma=False)
```

```python
import functools
import jax
import jax.numpy as jnp
from jax import lax
from jax.experimental import pallas as pl
from jax.experimental.pallas import tpu as pltpu
from jax.sharding import PartitionSpec as P

AXES = ("row", "col")
RING = 6
VMEM_LIMIT = 20 * 1024 * 1024


def tied(value, *others):
    return lax.optimization_barrier((value,) + others)[0]


def across(value, row, column, row_count, col_count):
    known = col_count - 1
    for bit in range(col_count.bit_length() - 2, 0, -1):
        received = lax.ppermute(value, AXES, spread_pairs(bit, known, row_count, col_count))
        known &= ~(1 << bit)
        value = jnp.where(((row ^ column) >> bit) & 1 == 0, value, received)
    return value


def exchanged(value, known, row_count, col_count):
    pieces = [value]
    for bit in range(col_count.bit_length() - 1, row_count.bit_length() - 1):
        pieces = pieces + [
            lax.ppermute(piece, AXES, spread_pairs(bit, known, row_count, col_count)) for piece in pieces
        ]
    return pieces


def spread_pairs(bit, known, row_count, col_count):
    chosen = []
    for source in range(row_count):
        for place in range(col_count):
            if (source ^ place) & known == 0:
                chosen.append((source * col_count + place, (source ^ (1 << bit)) * col_count + place))
    return chosen


def gather_and_spread(half, early, row, column, row_count, col_count):
    sizes = (row_count, col_count)

    def forward(part):
        value = across(part, row, column, *sizes)
        return exchanged(value, 1, *sizes)

    def to_other_core(near):
        return lax.ppermute(near, AXES, spread_pairs(0, 1, *sizes))

    def z_pairs(hops, wanted):
        return [
            (place * col_count + source, place * col_count + target)
            for place in range(row_count)
            for source, target in hops
            if (place % col_count == target) == wanted
        ]

    parts = [half]
    for mask in range(1, min(col_count, 3)):
        parts.append(lax.ppermute(half, "col", [(place, place ^ mask) for place in range(col_count)]))
    pieces = [forward(tied(half, early))]
    if col_count == 4:
        outer, inner = [(1, 0), (2, 3)], [(1, 2), (2, 1)]
        at_end = (column == 0) | (column == 3)
        near = [jnp.concatenate(pieces[0], 0)]
        middle = lax.ppermute(tied(half, parts[2]), AXES, z_pairs(inner, True))
        onward = lax.ppermute(parts[2], AXES, z_pairs(outer, True))
        first = jnp.where(at_end, onward, middle)
        turned = jnp.concatenate(exchanged(tied(parts[2], parts[1], pieces[0][-1]), col_count - 1, *sizes), 0)
        pieces.append(forward(parts[1]))
        middle = lax.ppermute(tied(half, parts[1], parts[2]), AXES, z_pairs(inner, False))
        onward = lax.ppermute(tied(parts[2], parts[1]), AXES, z_pairs(outer, False))
        near.append(jnp.concatenate(pieces[1], 0))
        near.append(across(tied(turned, first), row, column, *sizes))
        near.append(jnp.concatenate(forward(first), 0))
        parts += [first, onward, middle]
        near[1] = tied(near[1], onward, middle)
        near[3] = tied(near[3], near[2])
        far = [to_other_core(held) for held in near]
    else:
        for mask in range(len(parts), col_count):
            parts.append(lax.ppermute(half, "col", [(place, place ^ mask) for place in range(col_count)]))
        pieces += [forward(part) for part in parts[1:]]
        near = [jnp.concatenate(held, 0) for held in pieces]
        far = [to_other_core(held) for held in near]
    return parts, near, far


def renew_kernel(sizes, source_list, cell_list, *refs):
    col_count, groups, row_local, part_rows, slot_count, count, batch, ring = sizes
    part_count = len(refs) - 2 * col_count - 10
    row_parts, refs = refs[:part_count], refs[part_count:]
    col_near, refs = refs[:col_count], refs[col_count:]
    col_far, refs = refs[:col_count], refs[col_count:]
    tiles, out, row_buf, col_buf, in_buf, out_buf, row_sem, col_sem, in_sem, out_sem = refs
    tile_size = tiles.shape[1]
    steps = count // batch
    row = lax.axis_index("row")
    column = lax.axis_index("col")

    def fetch(step, slot):
        for t in range(batch):
            chosen = jnp.clip(source_list[step * batch + t], 0, slot_count - 1)
            pltpu.make_async_copy(tiles.at[chosen], in_buf.at[slot, t], in_sem.at[slot]).start()

    def cell(index):
        chosen = jnp.clip(source_list[index], 0, slot_count - 1)
        at_col = jnp.maximum(cell_list[1, chosen], 0)
        return jnp.maximum(cell_list[0, chosen], 0), lax.rem(at_col, groups), at_col // groups

    def stage(source, target, at, sem):
        pltpu.make_async_copy(source, target.at[pl.ds(pl.multiple_of(at, part_rows), part_rows)], sem).start()

    leads = lax.rem(row, col_count) == column
    at_end = (column == 0) | (column == col_count - 1)
    cases = (leads, jnp.logical_not(leads) & at_end, jnp.logical_not(leads | at_end))
    row_entries = [(entry, mask, None) for mask, entry in enumerate(row_parts[:col_count])]
    if part_count > col_count:
        last = col_count - 1
        row_entries = row_entries[:last] + [(entry, last, case) for entry, case in zip(row_parts[last:], cases)]
    is_near = (row ^ column) & 1 == 0

    def stage_all():
        for entry, mask, case in row_entries:
            @pl.when(True if case is None else case)
            def _(entry=entry, mask=mask):
                stage(entry, row_buf, (column ^ mask) * part_rows, row_sem)

        for held, wanted in ((col_near, is_near), (col_far, jnp.logical_not(is_near))):
            @pl.when(wanted)
            def _(held=held):
                for mask in range(col_count):
                    for piece in range(groups):
                        group = (row // col_count) ^ piece
                        at = (group * col_count + (column ^ mask)) * part_rows
                        stage(held[mask].at[pl.ds(piece * part_rows, part_rows)], col_buf, at, col_sem)

    early = min(2, ring, steps)
    for step in range(early):
        fetch(step, step)
    stage_all()
    for step in range(early, min(ring, steps)):
        fetch(step, step)
    pltpu.make_async_copy(row_buf, row_buf, row_sem).wait()
    pltpu.make_async_copy(col_buf, col_buf, col_sem).wait()

    def body(step, carry):
        slot = lax.rem(step, ring)
        pltpu.make_async_copy(in_buf.at[slot], in_buf.at[slot], in_sem.at[slot]).wait()

        @pl.when(step >= ring)
        def _():
            pltpu.make_async_copy(out_buf.at[slot], out_buf.at[slot], out_sem.at[slot]).wait()

        for t in range(batch):
            source = source_list[step * batch + t]
            at_row, group, at_col = cell(step * batch + t)
            at_flat = group * row_local + at_col
            left = row_buf[pl.ds(pl.multiple_of(at_row * tile_size, tile_size), tile_size), :]
            right = col_buf[pl.ds(pl.multiple_of(at_flat * tile_size, tile_size), tile_size), :]
            product = lax.dot_general(left, right, (((1,), (1,)), ((), ())), preferred_element_type=jnp.float32)
            fresh = in_buf[slot, t].astype(jnp.float32) - product
            out_buf[slot, t] = jnp.where(source >= 0, fresh, 0.0).astype(jnp.bfloat16)
        pltpu.make_async_copy(out_buf.at[slot], out.at[pl.ds(step * batch, batch)], out_sem.at[slot]).start()

        @pl.when(step + ring < steps)
        def _():
            fetch(step + ring, slot)

        return carry

    lax.fori_loop(0, steps, body, 0)
    for step in range(max(0, steps - ring), steps):
        slot = step % ring
        pltpu.make_async_copy(out_buf.at[slot], out_buf.at[slot], out_sem.at[slot]).wait()


def renew(source_list, cell_list, row_parts, col_near, col_far, tiles, groups, batch_most):
    slot_count, tile_size, _ = tiles.shape
    count = source_list.shape[0]
    part_rows = row_parts[0].shape[0]
    col_count = len(col_near)
    row_local = col_count * part_rows // tile_size
    batch = max(size for size in range(1, batch_most + 1) if count % size == 0)
    ring = min(RING, count // batch)
    sizes = (col_count, groups, row_local, part_rows, slot_count, count, batch, ring)
    operands = list(row_parts) + list(col_near) + list(col_far) + [tiles]
    tile_bytes = tile_size * tile_size * 2
    return pl.pallas_call(
        functools.partial(renew_kernel, sizes),
        out_shape=jax.ShapeDtypeStruct((count, tile_size, tile_size), jnp.bfloat16),
        grid_spec=pltpu.PrefetchScalarGridSpec(
            num_scalar_prefetch=2,
            grid=(),
            in_specs=[pl.BlockSpec(memory_space=pl.ANY)] * len(operands),
            out_specs=pl.BlockSpec(memory_space=pl.ANY),
            scratch_shapes=[
                pltpu.VMEM((row_local * tile_size, tile_size), jnp.bfloat16),
                pltpu.VMEM((groups * row_local * tile_size, tile_size), jnp.bfloat16),
                pltpu.VMEM((ring, batch, tile_size, tile_size), jnp.bfloat16),
                pltpu.VMEM((ring, batch, tile_size, tile_size), jnp.bfloat16),
                pltpu.SemaphoreType.DMA,
                pltpu.SemaphoreType.DMA,
                pltpu.SemaphoreType.DMA((ring,)),
                pltpu.SemaphoreType.DMA((ring,)),
            ],
        ),
        compiler_params=pltpu.CompilerParams(vmem_limit_bytes=VMEM_LIMIT),
        cost_estimate=pl.CostEstimate(
            flops=2 * count * tile_size**3,
            bytes_accessed=2 * count * tile_bytes + (1 + groups) * row_local * tile_bytes,
            transcendentals=0,
        ),
    )(source_list, cell_list, *operands)


def place_kernel(places, incoming, held, out, sem):
    del held
    count = incoming.shape[0]
    for index in range(count):
        @pl.when(places[index] >= 0)
        def _():
            pltpu.make_async_copy(incoming.at[index], out.at[places[index]], sem.at[index]).start()
    for index in range(count):
        @pl.when(places[index] >= 0)
        def _():
            pltpu.make_async_copy(incoming.at[index], out.at[places[index]], sem.at[index]).wait()


def place(places, incoming, held):
    return pl.pallas_call(
        place_kernel,
        out_shape=jax.ShapeDtypeStruct(held.shape, held.dtype),
        grid_spec=pltpu.PrefetchScalarGridSpec(
            num_scalar_prefetch=1,
            grid=(),
            in_specs=[pl.BlockSpec(memory_space=pltpu.VMEM), pl.BlockSpec(memory_space=pl.ANY)],
            out_specs=pl.BlockSpec(memory_space=pl.ANY),
            scratch_shapes=[pltpu.SemaphoreType.DMA((incoming.shape[0],))],
        ),
        input_output_aliases={2: 0},
        compiler_params=pltpu.CompilerParams(vmem_limit_bytes=4 * 1024 * 1024),
    )(places, incoming, held)


def shards(panel, diag_inverse, tiles, tile_map, send_list, place_list):
    slot_count = tiles.shape[0]
    move_count = send_list.shape[0]
    row_count = lax.axis_size("row")
    col_count = lax.axis_size("col")
    row = lax.axis_index("row")
    column = lax.axis_index("col")
    groups = row_count // col_count
    factor = jnp.dot(
        panel, diag_inverse.T, precision=lax.Precision.HIGH, preferred_element_type=jnp.float32
    )
    half = factor.astype(jnp.bfloat16)

    wanted = slot_count + jnp.arange(move_count, dtype=jnp.int32)
    spots = jnp.arange(place_list.shape[0], dtype=jnp.int32)
    places = jnp.max(jnp.where(place_list[None, :] == wanted[:, None], spots[None, :], -1), axis=1)

    row_parts, near, far = gather_and_spread(half, places, row, column, row_count, col_count)

    renewing = functools.partial(
        renew, cell_list=tile_map.T, row_parts=row_parts, col_near=near, col_far=far,
        tiles=tiles, groups=groups,
    )
    outgoing = renewing(send_list, batch_most=2)
    incoming = lax.ppermute(outgoing, "row", [(source, row_count - 1 - source) for source in range(row_count)])
    held = renewing(place_list, batch_most=8)
    balanced = place(places, incoming, held)
    return (factor, balanced)


def solution(mesh):
    in_specs = (
        P(("row", "col"), None),
        P(),
        P(("row", "col"), None, None),
        P(("row", "col"), None),
        P(("row", "col")),
        P(("row", "col")),
    )
    out_specs = (P(("row", "col"), None), P(("row", "col"), None, None))
    return jax.shard_map(shards, mesh=mesh, in_specs=in_specs, out_specs=out_specs, check_vma=False)
```
